256 devices in a mesh: dev: 64 (over x, z, core), tp: 4 (over y).
Axes of the slice: x: 4, y: 4, z: 8, core: 2. Of those that a mesh axis runs over, the one named last changes fastest.
Arguments:
- hidden: bfloat16 [512, 2, 7168], P('dev', None, 'tp'), may hold values from -6 to 6
- queries: bfloat16 [512, 2, 128, 576], P(('dev', 'tp'))
- latent_cache: bfloat16 [512, 256, 576], P(('dev', 'tp'))
- new_latent: bfloat16 [512, 2, 576], P(('dev', 'tp')), may hold values from -6 to 6
- lengths: int32 [512], P(('dev', 'tp')), may hold values from 17 to 256
- value_proj: bfloat16 [128, 512, 128], P('dev'), may hold values from -0.25 to 0.25
- out_proj: bfloat16 [16384, 7168], P('dev', 'tp'), may hold values from -0.046875 to 0.046875
- norm_gain: float32 [7168], P('tp'), may hold values from 0.1 to 1.9
- w_gate: bfloat16 [64, 7168, 1024], P('dev', None, 'tp'), may hold values from -0.0625 to 0.0625
- w_up: bfloat16 [64, 7168, 1024], P('dev', None, 'tp'), may hold values from -0.0625 to 0.0625
- w_down: bfloat16 [64, 1024, 7168], P('dev', 'tp'), may hold values from -0.1875 to 0.1875
- routes: int32 [512, 2, 8], P('dev'), may hold values from 0 to 63, all different within a row; in each aligned block of 16 rows (0 to 15, 16 to 31, ..., all dimensions but the last counted through in order) at most 4 rows name the same one
- route_gates: bfloat16 [512, 2, 8], P('dev'), may hold values from 0.049804688 to 0.44921875
Outputs:
- layer_out: bfloat16 [512, 2, 7168], P('dev', None, 'tp')
The draws below stay inside these ranges and needn't reach their ends.
Inputs may be any that keep to these rules, and one draw needn't show every extreme that they name: `routes`: among the 8 rows of one dev index, both steps taken together, no expert is named more than 4 times, a bound that some block reaches.
All inputs are finite; a program needn't handle non-finite values.
Results may differ from the reference program's by a relative error of at most 0.014.
Values may be sent and summed in bfloat16 or wider, within the bound.
No kernel may reach another device: no remote copies, remote signals or barrier semaphores. Data moves between devices by JAX's collectives and lax.ppermute only.
A program may use at most 128 MiB of HBM per device.

```python
import math
import jax
import jax.numpy as jnp
import numpy as np
from jax import lax

D = 7168
HEADS = 128
LAT = 512
ROPE = 64
VDIM = 128
TOP = 8
FF = 1024
STEPS = 2
ROWS_DEV = 2
CTX = 256
KV = 576
ROWS = 512
EXPERTS = 64
CAP = 4
N_DEV = 64
N_TP = 4


def shared_latents(key):
    return jax.random.normal(key, (ROWS, CTX, LAT + ROPE), jnp.float32)


def draw_latent_cache(key, part):
    base_latents = shared_latents(key)
    return base_latents.astype(jnp.bfloat16)


def draw_queries(key, part):
    key = jax.random.fold_in(key, 5)
    noise_key = jax.random.fold_in(key, 0)
    noise_part = jax.random.normal(noise_key, (ROWS, STEPS, HEADS, LAT + ROPE), jnp.float32)
    return noise_part.astype(jnp.bfloat16)


def draw_lengths(key, part):
    key = jax.random.fold_in(key, 7)
    scale_key, value_key, place_key = jax.random.split(key, 3)
    exponent = jax.random.randint(scale_key, (ROWS,), 0, 4)
    lower_end = jnp.right_shift(CTX, exponent + 1) + 1
    upper_end = jnp.right_shift(CTX, exponent) + 1
    drawn = jax.random.randint(value_key, (ROWS,), lower_end, upper_end)
    longest_at = jax.random.randint(place_key, (), 0, ROWS)
    return jnp.where(jnp.arange(ROWS) == longest_at, CTX, drawn).astype(jnp.int32)


def steps_of(rng, dims, cuts, least, top_value):
    gain, own = 1.0, jax.random.fold_in(rng, 6)
    for dim, shards_of in cuts:
        draws = jnp.exp(jax.random.uniform(jax.random.fold_in(own, dim), (shards_of,), jnp.float32, least / len(cuts), top_value / len(cuts)))
        gain = gain * jnp.repeat(draws, dims[dim] // shards_of).reshape([-1 if axis == dim else 1 for axis in range(len(dims))])
    return gain


def shared_out(rng, own, number, rows, amount, top, limit, lean):
    order = jax.random.permutation(rng, amount)
    heavy_load, ordinary = load_shares(amount, rows * top, limit, lean, True), load_shares(amount, rows * top, limit, lean, False)
    places = jnp.arange(amount)

    def named(sizes, rotation):
        used = int((sizes > 0).sum())
        fixed = max(1, used // 4)
        moved = fixed + (places - fixed + rotation * (used - fixed)) % max(1, amount - fixed)
        return jnp.zeros((amount,), jnp.int32).at[order[jnp.where(places < fixed, places, moved)]].set(jnp.asarray(sizes, jnp.int32))

    sizes = jnp.where(number % 4 == 0, named(heavy_load, number // 4), named(ordinary, number - number // 4 - 1))
    mixed = jax.random.permutation(jax.random.fold_in(own, 3), amount)
    source_of, taker = mixed[0:amount // 2 * 2:2], mixed[1:amount // 2 * 2:2]
    room = jnp.minimum(sizes[source_of] - 1, limit - sizes[taker]) // 2
    room = jnp.where((source_of == order[0]) | (taker == order[0]) | (sizes[taker] == 0), 0, jnp.maximum(room, 0))
    moved = jax.random.randint(jax.random.fold_in(own, 4), (amount // 2,), 0, 1 << 20) % (room + 1)
    sizes = sizes.at[source_of].add(-moved).at[taker].add(moved)
    labels = jnp.searchsorted(jnp.cumsum(sizes), jnp.arange(rows * top), side="right").astype(jnp.int32)
    listing = labels.reshape(top, rows).T
    listing = listing[jax.random.permutation(jax.random.fold_in(own, 1), rows)]
    rotation = jax.random.randint(jax.random.fold_in(own, 2), (rows, 1), 0, top)
    return jnp.take_along_axis(listing, (jnp.arange(top)[None, :] + rotation) % top, axis=1)


def load_shares(amount, total, most, skew, full):
    weights = [(1 << 20) // math.isqrt(standing ** skew) + 1 for standing in range(1, amount + 1)]
    largest = most if full else min(most, max(-(-total // amount), total * weights[0] // sum(weights)))
    least = 1 if total - largest >= amount - 1 else 0
    holding, rest = [largest] + [least] * (amount - 1), total - largest - least * (amount - 1)
    while rest > 0:
        movable = [i for i in range(1, amount) if holding[i] < largest] or [i for i in range(1, amount) if holding[i] < most]
        pool, remaining = sum([weights[i] for i in movable]), rest
        for i in movable:
            addition = min(most - holding[i], max(1, remaining * weights[i] // pool), rest)
            holding[i] = holding[i] + addition
            rest = rest - addition
    return np.array(holding)


def bell_draw(rng, dims, width, reach, cuts=(), held_as=jnp.bfloat16):
    result = jax.random.normal(rng, dims, jnp.float32) * width
    if len(cuts) > 0:
        result = steps_of(rng, dims, cuts, -0.22, 0.18) * result
    return jnp.clip(result, min=-reach, max=reach).astype(held_as)


def setup_inputs(seed: int = 0) -> dict:
    keys = jax.random.split(jax.random.key(seed), 14)
    hidden = bell_draw(keys[0], (ROWS, STEPS, D), 1.0, 6.0, ((0, 64), (2, 4)))
    queries = draw_queries(jax.random.fold_in(keys[13], 71), 0)
    latent_cache = draw_latent_cache(jax.random.fold_in(keys[13], 71), 0)
    new_latent = bell_draw(keys[3], (ROWS, STEPS, KV), 1.0, 6.0, ((0, 256),))
    lengths = draw_lengths(jax.random.fold_in(keys[13], 71), 0)
    value_proj = bell_draw(keys[5], (HEADS, LAT, VDIM), LAT ** -0.5, 0.25, ((0, 64),))
    out_proj = bell_draw(keys[6], (HEADS * VDIM, D), (HEADS * VDIM) ** -0.5, 0.046875, ((0, 64), (1, 4)))
    norm_gain = jnp.clip(1.0 + 0.18 * jax.random.normal(keys[7], (D,), jnp.float32), 0.1, 1.9)
    w_gate = bell_draw(keys[8], (EXPERTS, D, FF), D ** -0.5, 0.0625, ((0, 64), (2, 4)))
    w_up = bell_draw(keys[9], (EXPERTS, D, FF), D ** -0.5, 0.0625, ((0, 64), (2, 4)))
    w_down = bell_draw(keys[10], (EXPERTS, FF, D), FF ** -0.5, 0.1875, ((0, 64), (1, 4)))
    routes_keys = jax.random.split(jax.random.fold_in(keys[11], 1), ROWS * STEPS // (ROWS_DEV * N_TP * STEPS))
    routes_turns = jax.random.permutation(jax.random.fold_in(keys[11], 3), ROWS * STEPS // (ROWS_DEV * N_TP * STEPS))
    routes = jax.vmap(lambda own, number: shared_out(jax.random.fold_in(keys[11], 2), own, number, ROWS_DEV * N_TP * STEPS, EXPERTS, TOP, CAP, 2))(routes_keys, routes_turns).reshape((ROWS, STEPS, TOP))
    route_gates = jnp.clip(0.049804688 + 0.39941406 * jax.random.uniform(keys[12], (ROWS, STEPS, TOP), jnp.float32) ** steps_of(keys[12], (ROWS, STEPS, TOP), ((0, 64),), -0.2, 0.2), 0.049804688, 0.44921875).astype(jnp.bfloat16)
    return dict(hidden=hidden, queries=queries, latent_cache=latent_cache, new_latent=new_latent, lengths=lengths, value_proj=value_proj, out_proj=out_proj, norm_gain=norm_gain, w_gate=w_gate, w_up=w_up, w_down=w_down, routes=routes, route_gates=route_gates)


def attend_rows(query_rows, latent_rows, new_rows, row_lengths):
    key_rows = jnp.concatenate([latent_rows, new_rows], axis=1).astype(jnp.float32)
    scores = jnp.einsum('nshk,nck->nshc', query_rows.astype(jnp.float32), key_rows) * (VDIM + ROPE) ** (-0.5)
    position = jnp.arange(CTX + STEPS)
    step_index = jnp.arange(STEPS)
    cached = position[None, None, :] < row_lengths[:, None, None]
    new_allowed = position[None, :] - CTX <= step_index[:, None]
    allowed = jnp.where(position[None, None, :] < CTX, cached, new_allowed[None, :, :])
    scores = jnp.where(allowed[:, :, None, :], scores, -jnp.inf)
    probabilities = jax.nn.softmax(scores, axis=-1).astype(jnp.bfloat16)
    return jnp.einsum('nshc,ncl->nshl', probabilities.astype(jnp.float32), key_rows[:, :, :LAT]).astype(jnp.bfloat16)

def run_expert(operands):
    tokens_in, gate_mat, up_mat, down_mat = operands
    gate_out = jnp.dot(tokens_in, gate_mat, preferred_element_type=jnp.float32)
    up_out = jnp.dot(tokens_in, up_mat, preferred_element_type=jnp.float32)
    activation = (jax.nn.silu(gate_out) * up_out).astype(jnp.bfloat16)
    return jnp.dot(activation, down_mat, preferred_element_type=jnp.float32).astype(jnp.bfloat16)

def reference(hidden, queries, latent_cache, new_latent, lengths, value_proj, out_proj, norm_gain, w_gate, w_up, w_down, routes, route_gates):
    block_rows = 32
    blocks = ROWS // block_rows

    def attend_block(operands):
        return attend_rows(*operands)
    context = lax.map(attend_block, (queries.reshape(blocks, block_rows, STEPS, HEADS, LAT + ROPE), latent_cache.reshape(blocks, block_rows, CTX, LAT + ROPE), new_latent.reshape(blocks, block_rows, STEPS, LAT + ROPE), lengths.reshape(blocks, block_rows))).reshape(ROWS, STEPS, HEADS, LAT)
    head_values = jnp.einsum('nshl,hlv->nshv', context.astype(jnp.float32), value_proj.astype(jnp.float32)).astype(jnp.bfloat16)
    attention = jnp.dot(head_values.reshape(ROWS * STEPS, HEADS * VDIM), out_proj, preferred_element_type=jnp.float32)
    attention = attention.astype(jnp.bfloat16).reshape(ROWS, STEPS, D)
    residual = hidden.astype(jnp.float32) + attention.astype(jnp.float32)
    normed = residual * lax.rsqrt(lax.optimization_barrier(jnp.mean(residual * residual, axis=-1, keepdims=True)) + 1e-06) * norm_gain
    normed = normed.astype(jnp.bfloat16)
    groups = N_DEV
    pair_count = ROWS * STEPS * TOP // groups
    expert_ids = routes.reshape(groups, pair_count)
    ordinal = jnp.arange(pair_count)
    same_expert = (expert_ids[:, :, None] == expert_ids[:, None, :]) & (ordinal[None, None, :] < ordinal[None, :, None])
    slot_index = lax.optimization_barrier(jnp.sum(same_expert.astype(jnp.int32), axis=2)).astype(jnp.int32)
    column = (jnp.arange(groups)[:, None] * CAP + slot_index).astype(jnp.int32)
    tokens = normed.reshape(groups, pair_count // TOP, D)
    source = tokens[:, ordinal // TOP, :]
    inputs = jnp.zeros((EXPERTS, groups * CAP, D), jnp.bfloat16).at[expert_ids, column].set(source)
    outputs = lax.map(run_expert, (inputs, w_gate, w_up, w_down))
    picked = outputs[expert_ids, column].astype(jnp.float32)
    weighted = picked * route_gates.reshape(groups, pair_count).astype(jnp.float32)[:, :, None]
    mixture = lax.optimization_barrier(jnp.sum(weighted.reshape(groups, pair_count // TOP, TOP, D), axis=2)).reshape(ROWS, STEPS, D)
    return (residual + mixture).astype(jnp.bfloat16)
```

```python
import jax
import jax.numpy as jnp
from jax import lax
from jax.sharding import Mesh, PartitionSpec as P

EPS = 1e-06
CAP = 4
NC = 2
F32 = jnp.float32
BF16 = jnp.bfloat16
CHIPS = ("x", "z")


def swap(value):
    return lax.ppermute(value, "c", [(0, 1), (1, 0)])


def send_y(value, distance):
    size = lax.axis_size("y")
    return lax.ppermute(value, "y", [(i, (i + distance) % size) for i in range(size)])


def in_core_order(core, own, other, axis=0):
    first = jnp.where(core == 0, own, other)
    second = jnp.where(core == 0, other, own)
    return jnp.concatenate([first, second], axis=axis)


def attend(queries, cache, new_latent, lengths, lat, scale):
    steps = queries.shape[1]
    scores = jnp.einsum("nshk,nck->nshc", queries, cache, preferred_element_type=F32) * scale
    fresh = jnp.einsum("nshk,njk->nshj", queries, new_latent, preferred_element_type=F32) * scale
    seen = jnp.arange(cache.shape[1])[None, :] < lengths[:, None]
    scores = jnp.where(seen[:, None, None, :], scores, -jnp.inf)
    known = jnp.arange(steps)[None, :] <= jnp.arange(steps)[:, None]
    fresh = jnp.where(known[None, :, None, :], fresh, -jnp.inf)
    top = jnp.maximum(jnp.max(scores, axis=-1), jnp.max(fresh, axis=-1))[..., None]
    scores = jnp.exp(scores - top)
    fresh = jnp.exp(fresh - top)
    total = (jnp.sum(scores, axis=-1) + jnp.sum(fresh, axis=-1))[..., None]
    old_part = jnp.einsum(
        "nshc,ncl->nshl", (scores / total).astype(BF16), cache[:, :, :lat], preferred_element_type=F32
    )
    new_part = jnp.einsum(
        "nshj,njl->nshl", (fresh / total).astype(BF16), new_latent[:, :, :lat], preferred_element_type=F32
    )
    return (old_part + new_part).astype(BF16)


def slots_of(ids):
    flat = ids.reshape(-1)
    order = jnp.arange(flat.shape[0])
    earlier = (flat[:, None] == flat[None, :]) & (order[None, :] < order[:, None])
    return jnp.sum(earlier.astype(jnp.int32), axis=1).reshape(ids.shape)


def on_device(
    hidden,
    queries,
    latent_cache,
    new_latent,
    lengths,
    value_proj,
    out_proj,
    norm_gain,
    w_gate,
    w_up,
    w_down,
    routes,
    route_gates,
):
    core = lax.axis_index("c")
    y = lax.axis_index("y")
    ny = lax.axis_size("y")
    chips = lax.axis_size("x") * lax.axis_size("z")
    rows, steps, heads, kv = queries.shape
    heads_core, lat, vdim = value_proj.shape
    rope = kv - lat
    cols = hidden.shape[2]
    half = cols // NC
    width = cols * ny
    own_tokens = rows * steps
    group = own_tokens * ny
    heads_chip = heads_core * NC

    def half_of(value, which):
        return lax.dynamic_slice_in_dim(value, which * half, half, value.ndim - 1)

    vp = in_core_order(core, value_proj, swap(value_proj))
    op = in_core_order(core, half_of(out_proj, core), swap(half_of(out_proj, 1 - core)))
    flat_hidden = hidden.reshape(group, cols)
    chip_hidden = in_core_order(
        core, half_of(flat_hidden, core)[None], swap(half_of(flat_hidden, 1 - core))[None]
    )
    ids = routes.reshape(group, -1)
    gates = route_gates.reshape(group, -1)
    chip_ids = in_core_order(core, ids[None], swap(ids)[None])
    chip_gates = in_core_order(core, gates[None], swap(gates)[None]).astype(F32)

    context = attend(queries, latent_cache, new_latent, lengths, lat, (vdim + rope) ** (-0.5))
    context = context.reshape(own_tokens, chips, heads_chip, lat).transpose(1, 0, 2, 3)
    context = lax.all_to_all(context, CHIPS, 0, 0, tiled=True)
    values = jnp.einsum("nthl,hlv->nthv", context, vp, preferred_element_type=F32).astype(BF16)
    values = values.reshape(chips, own_tokens, heads_chip * vdim)

    blocks = [values] + [send_y(values, d) for d in range(1, ny)]
    mine = jnp.stack(blocks, axis=1)
    both = jnp.stack([mine, swap(mine)], axis=1)

    down_own = w_down[0]

    def down_block(block):
        return lax.dynamic_slice_in_dim(down_own, (block % ny) * cols, cols, 1)

    near = (1, ny - 1)
    early = [send_y(down_block(y + d), d) for d in near]
    both, *early = lax.optimization_barrier((both, *early))
    partial_sums = jnp.dot(
        both.reshape(-1, heads_chip * vdim), op, preferred_element_type=F32
    ).astype(BF16)
    partial_sums = partial_sums.reshape(chips, NC * group, half)
    arrived = lax.all_to_all(partial_sums, CHIPS, 0, 0, tiled=True)
    attention = jnp.sum(arrived.astype(F32), axis=0).astype(BF16)
    attention = attention.reshape(NC, ny, own_tokens, half)
    core_order = (jnp.arange(NC) + core) % NC
    y_order = (y - jnp.arange(ny)) % ny
    attention = attention[core_order][:, y_order].reshape(NC, group, half)
    residual = chip_hidden.astype(F32) + attention.astype(F32)
    gain = half_of(norm_gain, core)
    scaled = (residual * gain).astype(BF16).reshape(NC * group, half)
    other_half = swap(lax.dynamic_index_in_dim(residual, 1 - core, 0, keepdims=False))
    own_half = lax.dynamic_index_in_dim(residual, core, 0, keepdims=False)
    full_residual = in_core_order(core, own_half, other_half, axis=1)

    chip_slots = jnp.stack([slots_of(chip_ids[0]), slots_of(chip_ids[1])])
    group_of = jnp.arange(NC)[:, None, None]
    row_of = (chip_ids * NC + group_of) * CAP + chip_slots
    row_of = row_of.reshape(NC * group, -1)
    row_count = chips * NC * NC * CAP
    named = row_of[:, :, None] == jnp.arange(row_count)[None, None, :]
    spread = jnp.sum(named.astype(F32), axis=1).astype(BF16)
    combine = jnp.sum(named.astype(F32) * chip_gates.reshape(NC * group, -1)[:, :, None], axis=1)
    combine = combine.astype(BF16).reshape(NC * group, chips, NC, NC * CAP)
    combine = lax.dynamic_index_in_dim(combine, core, 2, keepdims=False)
    outgoing = lax.dot_general(
        spread, scaled, (((0,), (0,)), ((), ())), preferred_element_type=F32
    ).astype(BF16)
    outgoing = outgoing.reshape(chips, NC * NC * CAP, half)
    tokens = lax.all_to_all(outgoing, CHIPS, 0, 0, tiled=True)
    tokens = tokens.reshape(chips, NC, NC * CAP, half)
    kept = lax.dynamic_index_in_dim(tokens, core, 1, keepdims=False)
    received = swap(lax.dynamic_index_in_dim(tokens, 1 - core, 1, keepdims=False))
    slots = chips * NC * CAP
    tokens = in_core_order(core, kept.reshape(slots, half), received.reshape(slots, half), axis=1)

    gate_w, up_w, down_own, _ = lax.optimization_barrier((w_gate[0], w_up[0], down_own, mine))

    def up_block(block):
        start = (block % ny) * cols
        return jnp.concatenate(
            [
                lax.dynamic_slice_in_dim(gate_w, start, cols, 0),
                lax.dynamic_slice_in_dim(up_w, start, cols, 0),
            ],
            axis=1,
        )

    up_parts = [up_block(y)] + [send_y(up_block(y + d), d) for d in range(1, ny)]
    down_parts = {0: down_block(y), **dict(zip(near, early))}
    for d in range(1, ny):
        if d not in near:
            down_parts[d] = send_y(down_block(y + d), d)

    column_gain = norm_gain
    shares = jnp.sum(jnp.square(tokens.astype(F32) / column_gain), axis=1)
    squares = shares
    for d in range(1, ny):
        squares = squares + send_y(shares, d)
    row_scale = lax.rsqrt(squares / width + EPS)[:, None]
    sums = jnp.dot(tokens, up_parts[0], preferred_element_type=F32)
    for d in range(1, ny):
        part = jnp.dot(tokens, up_parts[d], preferred_element_type=F32).astype(BF16)
        sums = sums + send_y(part, -d).astype(F32)
    sums = sums * row_scale
    units = sums.shape[1] // 2
    act = (jax.nn.silu(sums[:, :units]) * sums[:, units:]).astype(BF16)
    result = jnp.dot(act, down_parts[0], preferred_element_type=F32)
    for d in range(1, ny):
        result = result + jnp.dot(send_y(act, d), down_parts[d], preferred_element_type=F32)
    result = result.astype(BF16).reshape(chips, NC * CAP, cols)

    returned = lax.all_to_all(result, CHIPS, 0, 0, tiled=True).reshape(slots, cols)
    mixture = jnp.dot(
        combine.reshape(NC * group, slots), returned, preferred_element_type=F32
    ).reshape(NC, group, cols)
    mixture_own = lax.dynamic_index_in_dim(mixture, core, 0, keepdims=False)
    mixture_other = swap(lax.dynamic_index_in_dim(mixture, 1 - core, 0, keepdims=False))
    layer_out = full_residual + (mixture_own + mixture_other)
    return layer_out.astype(BF16).reshape(hidden.shape)


def split_mesh(mesh, nz):
    dev_count, y_count = mesh.devices.shape
    nx = dev_count // (NC * nz)
    return Mesh(mesh.devices.reshape(nx, nz, NC, y_count), ("x", "z", "c", "y"))


def solution(mesh, nz=8):
    dev = ("x", "z", "c")
    both = ("x", "z", "c", "y")
    in_specs = (
        P(dev, None, "y"),
        P(both, None, None, None),
        P(both, None, None),
        P(both, None, None),
        P(both),
        P(dev, None, None),
        P(dev, "y"),
        P("y"),
        P(dev, None, "y"),
        P(dev, None, "y"),
        P(dev, "y", None),
        P(dev, None, None),
        P(dev, None, None),
    )
    return jax.shard_map(
        on_device,
        mesh=split_mesh(mesh, nz),
        in_specs=in_specs,
        out_specs=P(dev, None, "y"),
        check_vma=False,
    )
```

```python
import jax
import jax.numpy as jnp
from jax import lax
from jax.sharding import Mesh, PartitionSpec as P

EPS = 1e-06
CAP = 4
NC = 2
F32 = jnp.float32
BF16 = jnp.bfloat16
CHIPS = ("x", "z")


def swap(value):
    return lax.ppermute(value, "c", [(0, 1), (1, 0)])


def send_y(value, distance):
    size = lax.axis_size("y")
    return lax.ppermute(value, "y", [(i, (i + distance) % size) for i in range(size)])


def in_core_order(core, own, other, axis=0):
    first = jnp.where(core == 0, own, other)
    second = jnp.where(core == 0, other, own)
    return jnp.concatenate([first, second], axis=axis)


def attend(queries, cache, new_latent, lengths, lat, scale):
    steps = queries.shape[1]
    scores = jnp.einsum("nshk,nck->nshc", queries, cache, preferred_element_type=F32) * scale
    fresh = jnp.einsum("nshk,njk->nshj", queries, new_latent, preferred_element_type=F32) * scale
    seen = jnp.arange(cache.shape[1])[None, :] < lengths[:, None]
    scores = jnp.where(seen[:, None, None, :], scores, -jnp.inf)
    known = jnp.arange(steps)[None, :] <= jnp.arange(steps)[:, None]
    fresh = jnp.where(known[None, :, None, :], fresh, -jnp.inf)
    top = jnp.maximum(jnp.max(scores, axis=-1), jnp.max(fresh, axis=-1))[..., None]
    scores = jnp.exp(scores - top)
    fresh = jnp.exp(fresh - top)
    total = (jnp.sum(scores, axis=-1) + jnp.sum(fresh, axis=-1))[..., None]
    old_part = jnp.einsum(
        "nshc,ncl->nshl", (scores / total).astype(BF16), cache[:, :, :lat], preferred_element_type=F32
    )
    new_part = jnp.einsum(
        "nshj,njl->nshl", (fresh / total).astype(BF16), new_latent[:, :, :lat], preferred_element_type=F32
    )
    return (old_part + new_part).astype(BF16)


def slots_of(ids):
    flat = ids.reshape(-1)
    order = jnp.arange(flat.shape[0])
    earlier = (flat[:, None] == flat[None, :]) & (order[None, :] < order[:, None])
    return jnp.sum(earlier.astype(jnp.int32), axis=1).reshape(ids.shape)


def on_device(
    hidden,
    queries,
    latent_cache,
    new_latent,
    lengths,
    value_proj,
    out_proj,
    norm_gain,
    w_gate,
    w_up,
    w_down,
    routes,
    route_gates,
):
    core = lax.axis_index("c")
    y = lax.axis_index("y")
    ny = lax.axis_size("y")
    chips = lax.axis_size("x") * lax.axis_size("z")
    rows, steps, heads, kv = queries.shape
    heads_core, lat, vdim = value_proj.shape
    rope = kv - lat
    cols = hidden.shape[2]
    half = cols // NC
    units = w_gate.shape[2]
    width = cols * ny
    own_tokens = rows * steps
    group = own_tokens * ny
    heads_chip = heads_core * NC
    slots = chips * NC * CAP
    near = (1, ny - 1)
    far = tuple(d for d in range(1, ny) if d not in near)

    def half_of(value, which):
        return lax.dynamic_slice_in_dim(value, which * half, half, value.ndim - 1)

    def after(value, done):
        return lax.optimization_barrier((value, done))[0]

    def over_chips(value):
        return lax.all_to_all(value, CHIPS, 0, 0, tiled=True)

    def down_block(block):
        return lax.dynamic_slice_in_dim(w_down[0], (block % ny) * cols, cols, 1)

    def row_block(weight, block):
        return lax.dynamic_slice_in_dim(weight[0], (block % ny) * cols, cols, 0)

    def up_block(block):
        return jnp.concatenate([row_block(w_gate, block), row_block(w_up, block)], axis=1)

    def half_block(block, which):
        start = (block % ny) * cols + which * half
        return jnp.concatenate(
            [lax.dynamic_slice_in_dim(weight[0], start, half, 0) for weight in (w_gate, w_up)],
            axis=1,
        )

    down_parts = {d: send_y(down_block(y + d), d) for d in near}
    near_up = {d: up_block(y + d) for d in near}
    far_gain = {d: send_y(norm_gain, d) for d in far}

    vp = in_core_order(core, value_proj, swap(value_proj))
    op = in_core_order(core, half_of(out_proj, core), swap(half_of(out_proj, 1 - core)))
    flat_hidden = hidden.reshape(group, cols)
    chip_hidden = in_core_order(
        core, half_of(flat_hidden, core)[None], swap(half_of(flat_hidden, 1 - core))[None]
    )
    ids = routes.reshape(group, -1)
    gates = route_gates.reshape(group, -1)
    chip_ids = in_core_order(core, ids[None], swap(ids)[None])
    chip_gates = in_core_order(core, gates[None], swap(gates)[None]).astype(F32)

    context = attend(queries, latent_cache, new_latent, lengths, lat, (vdim + rope) ** (-0.5))
    context = context.reshape(own_tokens, chips, heads_chip, lat).transpose(1, 0, 2, 3)
    context = over_chips(context)
    context, down_parts, near_up, vp, op, far_gain = lax.optimization_barrier(
        (context, down_parts, near_up, vp, op, far_gain)
    )
    values = jnp.einsum("nthl,hlv->nthv", context, vp, preferred_element_type=F32).astype(BF16)

    values = jnp.concatenate([values] + [send_y(values, d) for d in range(1, ny)], axis=1)
    up_parts = {d: send_y(block, d) for d, block in after(near_up, values).items()}
    values = values.reshape(chips, group, heads_chip * vdim)
    values = jnp.concatenate([values, swap(values)], axis=1)
    sums = jnp.dot(
        values.reshape(-1, heads_chip * vdim), op, preferred_element_type=F32
    ).astype(BF16)
    sums = over_chips(sums.reshape(chips, NC * group, half))
    sums = jnp.sum(sums.astype(F32), axis=0).astype(BF16).astype(F32)

    core_order = (core + jnp.arange(NC)) % NC
    y_order = (y - jnp.arange(ny)) % ny
    token = jnp.arange(own_tokens)
    place = core_order[:, None, None] * group + y_order[None, :, None] * own_tokens + token
    place = place.reshape(-1)
    placed_hidden = chip_hidden.reshape(NC * group, half)[place].astype(F32)
    gain = half_of(norm_gain, core)

    chip_slots = jnp.stack([slots_of(chip_ids[0]), slots_of(chip_ids[1])])
    group_of = jnp.arange(NC)[:, None, None]
    row_of = (chip_ids * NC + group_of) * CAP + chip_slots
    row_of = row_of.reshape(NC * group, -1)
    row_ids = jnp.arange(chips * NC * NC * CAP)[None, None, :]
    named = row_of[:, :, None] == row_ids
    weighted = named.astype(F32) * chip_gates.reshape(NC * group, -1)[:, :, None]
    combine = jnp.sum(weighted, axis=1).astype(BF16).reshape(NC * group, chips, NC, NC * CAP)
    combine = lax.dynamic_index_in_dim(combine, core, 2, keepdims=False)
    spread = jnp.sum((row_of[place][:, :, None] == row_ids).astype(F32), axis=1).astype(BF16)

    residual = placed_hidden + sums
    scaled = (residual * gain).astype(BF16)
    far_down = {d: send_y(after(down_block(y + d), up_parts), d) for d in far}
    outgoing = lax.dot_general(
        spread, scaled, (((0,), (0,)), ((), ())), preferred_element_type=F32
    ).astype(BF16)
    tokens = over_chips(outgoing.reshape(chips, NC * NC * CAP, half))
    tokens = tokens.reshape(chips, NC, NC * CAP, half)
    kept = lax.dynamic_index_in_dim(tokens, core, 1, keepdims=False).reshape(slots, half)
    received = swap(lax.dynamic_index_in_dim(tokens, 1 - core, 1, keepdims=False))
    received = received.reshape(slots, half)
    kept, far_down = lax.optimization_barrier((kept, far_down))
    far_tokens = {d: (send_y(kept, d), send_y(received, d)) for d in far}
    down_parts.update(far_down)
    down_parts[0] = down_block(y)
    tokens = in_core_order(core, kept, received, axis=1)

    residual = residual.reshape(NC, group, half)
    full_residual = in_core_order(core, residual[0], swap(residual[1]), axis=1)
    back = (y - jnp.arange(ny)) % ny
    full_residual = full_residual.reshape(ny, own_tokens, cols)[back].reshape(group, cols)

    def share(part, gains):
        return jnp.sum(jnp.square(part.astype(F32) / gains), axis=1, keepdims=True)

    own_share = share(tokens, norm_gain)
    coarse = lax.reduce_precision(own_share, 8, 7)
    lanes = jnp.arange(128)[None, :]
    share_lanes = jnp.where(lanes == 0, coarse, jnp.where(lanes == 1, own_share - coarse, 0.0))
    squares = own_share
    sums = jnp.dot(tokens, up_block(y), preferred_element_type=F32)
    for d in near:
        part = jnp.dot(tokens, up_parts[d], preferred_element_type=F32)
        part = jnp.concatenate([part.astype(BF16), share_lanes.astype(BF16)], axis=1)
        part = send_y(part, -d).astype(F32)
        sums = sums + part[:, : 2 * units]
        squares = squares + part[:, 2 * units : 2 * units + 1]
        squares = squares + part[:, 2 * units + 1 : 2 * units + 2]
    for d in far:
        for part, which in zip(far_tokens[d], (core, 1 - core)):
            sums = sums + jnp.dot(part, half_block(y - d, which), preferred_element_type=F32)
            squares = squares + share(part, half_of(far_gain[d], which))
    sums = sums * lax.rsqrt(squares / width + EPS)
    act = (jax.nn.silu(sums[:, :units]) * sums[:, units:]).astype(BF16)
    acts = {0: act, **{d: send_y(act, d) for d in near + far}}
    result = sum(
        jnp.dot(acts[d], down_parts[d], preferred_element_type=F32) for d in (0,) + near + far
    )
    result = result.astype(BF16).reshape(chips, NC * CAP, cols)

    returned = over_chips(result).reshape(slots, cols)
    mixture = jnp.dot(
        combine.reshape(NC * group, slots), returned, preferred_element_type=F32
    ).reshape(NC, group, cols)
    mixture_own = lax.dynamic_index_in_dim(mixture, core, 0, keepdims=False)
    mixture_other = swap(lax.dynamic_index_in_dim(mixture, 1 - core, 0, keepdims=False))
    layer_out = full_residual + (mixture_own + mixture_other)
    return layer_out.astype(BF16).reshape(hidden.shape)


def split_mesh(mesh, nz):
    dev_count, y_count = mesh.devices.shape
    nx = dev_count // (NC * nz)
    return Mesh(mesh.devices.reshape(nx, nz, NC, y_count), ("x", "z", "c", "y"))


def solution(mesh, nz=8):
    dev = ("x", "z", "c")
    both = ("x", "z", "c", "y")
    in_specs = (
        P(dev, None, "y"),
        P(both, None, None, None),
        P(both, None, None),
        P(both, None, None),
        P(both),
        P(dev, None, None),
        P(dev, "y"),
        P("y"),
        P(dev, None, "y"),
        P(dev, None, "y"),
        P(dev, "y", None),
        P(dev, None, None),
        P(dev, None, None),
    )
    return jax.shard_map(
        on_device,
        mesh=split_mesh(mesh, nz),
        in_specs=in_specs,
        out_specs=P(dev, None, "y"),
        check_vma=False,
    )
```

```python
import jax
import jax.numpy as jnp
from jax import lax
from jax.sharding import Mesh, PartitionSpec as P

EPS = 1e-06
CAP = 4
NC = 2
F32 = jnp.float32
BF16 = jnp.bfloat16
CHIPS = ("x", "z")


def swap(value):
    return lax.ppermute(value, "c", [(0, 1), (1, 0)])


def send_y(value, distance):
    size = lax.axis_size("y")
    return lax.ppermute(value, "y", [(i, (i + distance) % size) for i in range(size)])


def in_core_order(core, own, other, axis=0):
    first = jnp.where(core == 0, own, other)
    second = jnp.where(core == 0, other, own)
    return jnp.concatenate([first, second], axis=axis)


def attend(queries, cache, new_latent, lengths, lat, scale):
    steps = queries.shape[1]
    scores = jnp.einsum("nshk,nck->nshc", queries, cache, preferred_element_type=F32) * scale
    fresh = jnp.einsum("nshk,njk->nshj", queries, new_latent, preferred_element_type=F32) * scale
    seen = jnp.arange(cache.shape[1])[None, :] < lengths[:, None]
    scores = jnp.where(seen[:, None, None, :], scores, -jnp.inf)
    known = jnp.arange(steps)[None, :] <= jnp.arange(steps)[:, None]
    fresh = jnp.where(known[None, :, None, :], fresh, -jnp.inf)
    top = jnp.maximum(jnp.max(scores, axis=-1), jnp.max(fresh, axis=-1))[..., None]
    scores = jnp.exp(scores - top)
    fresh = jnp.exp(fresh - top)
    total = (jnp.sum(scores, axis=-1) + jnp.sum(fresh, axis=-1))[..., None]
    old_part = jnp.einsum(
        "nshc,ncl->nshl", (scores / total).astype(BF16), cache[:, :, :lat], preferred_element_type=F32
    )
    new_part = jnp.einsum(
        "nshj,njl->nshl", (fresh / total).astype(BF16), new_latent[:, :, :lat], preferred_element_type=F32
    )
    return (old_part + new_part).astype(BF16)


def slots_of(ids):
    flat = ids.reshape(-1)
    order = jnp.arange(flat.shape[0])
    earlier = (flat[:, None] == flat[None, :]) & (order[None, :] < order[:, None])
    return jnp.sum(earlier.astype(jnp.int32), axis=1).reshape(ids.shape)


def on_device(
    hidden,
    queries,
    latent_cache,
    new_latent,
    lengths,
    value_proj,
    out_proj,
    norm_gain,
    w_gate,
    w_up,
    w_down,
    routes,
    route_gates,
):
    core = lax.axis_index("c")
    y = lax.axis_index("y")
    ny = lax.axis_size("y")
    chips = lax.axis_size("x") * lax.axis_size("z")
    rows, steps, heads, kv = queries.shape
    heads_core, lat, vdim = value_proj.shape
    rope = kv - lat
    cols = hidden.shape[2]
    half = cols // NC
    units = w_gate.shape[2]
    width = cols * ny
    own_tokens = rows * steps
    group = own_tokens * ny
    heads_chip = heads_core * NC
    slots = chips * NC * CAP
    near = (1, ny - 1)
    far = tuple(d for d in range(1, ny) if d not in near)

    def half_of(value, which):
        return lax.dynamic_slice_in_dim(value, which * half, half, value.ndim - 1)

    def after(value, done):
        return lax.optimization_barrier((value, done))[0]

    def over_chips(value):
        return lax.all_to_all(value, CHIPS, 0, 0, tiled=True)

    def down_block(block):
        return lax.dynamic_slice_in_dim(w_down[0], (block % ny) * cols, cols, 1)

    def row_block(weight, block):
        return lax.dynamic_slice_in_dim(weight[0], (block % ny) * cols, cols, 0)

    def up_block(block):
        return jnp.concatenate([row_block(w_gate, block), row_block(w_up, block)], axis=1)

    def half_block(block, which):
        start = (block % ny) * cols + which * half
        return jnp.concatenate(
            [lax.dynamic_slice_in_dim(weight[0], start, half, 0) for weight in (w_gate, w_up)],
            axis=1,
        )

    near_down = {d: send_y(down_block(y + d), d) for d in near}
    near_up = {d: up_block(y + d) for d in near}
    far_gain = {d: send_y(norm_gain, d) for d in far}

    vp = in_core_order(core, value_proj, swap(value_proj))
    op = in_core_order(core, half_of(out_proj, core), swap(half_of(out_proj, 1 - core)))
    flat_hidden = hidden.reshape(group, cols)
    chip_hidden = in_core_order(
        core, half_of(flat_hidden, core)[None], swap(half_of(flat_hidden, 1 - core))[None]
    )
    ids = routes.reshape(group, -1)
    gates = route_gates.reshape(group, -1)
    chip_ids = in_core_order(core, ids[None], swap(ids)[None])
    chip_gates = in_core_order(core, gates[None], swap(gates)[None]).astype(F32)

    context = attend(queries, latent_cache, new_latent, lengths, lat, (vdim + rope) ** (-0.5))
    context = context.reshape(own_tokens, chips, heads_chip, lat).transpose(1, 0, 2, 3)
    context = over_chips(context)
    context, near_down, near_up, vp, op, far_gain = lax.optimization_barrier(
        (context, near_down, near_up, vp, op, far_gain)
    )
    values = jnp.einsum("nthl,hlv->nthv", context, vp, preferred_element_type=F32).astype(BF16)

    values = jnp.concatenate([values] + [send_y(values, d) for d in range(1, ny)], axis=1)
    up_parts = {d: send_y(block, d) for d, block in after(near_up, values).items()}
    values = values.reshape(chips, group, heads_chip * vdim)
    values = jnp.concatenate([values, swap(values)], axis=1)
    sums = jnp.dot(
        values.reshape(-1, heads_chip * vdim), op, preferred_element_type=F32
    ).astype(BF16)
    sums = over_chips(sums.reshape(chips, NC * group, half))
    sums = jnp.sum(sums.astype(F32), axis=0).astype(BF16).astype(F32)

    core_order = (core + jnp.arange(NC)) % NC
    y_order = (y - jnp.arange(ny)) % ny
    token = jnp.arange(own_tokens)
    place = core_order[:, None, None] * group + y_order[None, :, None] * own_tokens + token
    place = place.reshape(-1)
    placed_hidden = chip_hidden.reshape(NC * group, half)[place].astype(F32)
    gain = half_of(norm_gain, core)

    chip_slots = jnp.stack([slots_of(chip_ids[0]), slots_of(chip_ids[1])])
    group_of = jnp.arange(NC)[:, None, None]
    row_of = ((chip_ids ^ core) * NC + group_of) * CAP + chip_slots
    row_of = row_of.reshape(NC * group, -1)
    row_ids = jnp.arange(chips * NC * NC * CAP)[None, None, :]
    named = row_of[:, :, None] == row_ids
    weighted = named.astype(F32) * chip_gates.reshape(NC * group, -1)[:, :, None]
    combine = jnp.sum(weighted, axis=1).astype(BF16).reshape(NC * group, chips, NC, NC * CAP)
    combine = combine[:, :, 0]
    spread = jnp.sum((row_of[place][:, :, None] == row_ids).astype(F32), axis=1).astype(BF16)

    residual = placed_hidden + sums
    scaled = (residual * gain).astype(BF16)
    far_down = {d: send_y(after(down_block(y + d), up_parts), d) for d in far}
    outgoing = lax.dot_general(
        spread, scaled, (((0,), (0,)), ((), ())), preferred_element_type=F32
    ).astype(BF16)
    tokens = over_chips(outgoing.reshape(chips, NC * NC * CAP, half))
    tokens = tokens.reshape(chips, NC, NC * CAP, half)
    kept, given = tokens[:, 0].reshape(slots, half), tokens[:, 1].reshape(slots, half)
    received = swap(given)
    kept, far_down = lax.optimization_barrier((kept, far_down))
    far_tokens = {d: (send_y(kept, d), swap(send_y(given, d))) for d in far}
    down_all = [down_block(y)] + [near_down[d] for d in near] + [far_down[d] for d in far]
    down_all = jnp.concatenate(down_all, axis=0)
    tokens = in_core_order(core, kept, received, axis=1)

    residual = residual.reshape(NC, group, half)
    full_residual = in_core_order(core, residual[0], swap(residual[1]), axis=1)
    back = (y - jnp.arange(ny)) % ny
    full_residual = full_residual.reshape(ny, own_tokens, cols)[back].reshape(group, cols)

    def share(part, gains):
        return jnp.sum(jnp.square(part.astype(F32) / gains), axis=1, keepdims=True)

    own_share = share(tokens, norm_gain)
    coarse = lax.reduce_precision(own_share, 8, 7)
    lanes = jnp.arange(128)[None, :]
    share_lanes = jnp.where(lanes == 0, coarse, jnp.where(lanes == 1, own_share - coarse, 0.0))
    squares = own_share
    sums = jnp.dot(tokens, up_block(y), preferred_element_type=F32)
    for d in near:
        part = jnp.dot(tokens, up_parts[d], preferred_element_type=F32)
        part = jnp.concatenate([part.astype(BF16), share_lanes.astype(BF16)], axis=1)
        part = send_y(part, -d).astype(F32)
        sums = sums + part[:, : 2 * units]
        squares = squares + part[:, 2 * units : 2 * units + 1]
        squares = squares + part[:, 2 * units + 1 : 2 * units + 2]
    for d in far:
        for part, which in zip(far_tokens[d], (core, 1 - core)):
            sums = sums + jnp.dot(part, half_block(y - d, which), preferred_element_type=F32)
            squares = squares + share(part, half_of(far_gain[d], which))
    sums = sums * lax.rsqrt(squares / width + EPS)
    act = (jax.nn.silu(sums[:, :units]) * sums[:, units:]).astype(BF16)
    acts = jnp.concatenate([act] + [send_y(act, d) for d in near + far], axis=1)
    result = jnp.dot(acts, down_all, preferred_element_type=F32)
    result = result.astype(BF16).reshape(chips, NC * CAP, cols)

    returned = over_chips(result).reshape(slots, cols)
    mixture = jnp.dot(
        combine.reshape(NC * group, slots), returned, preferred_element_type=F32
    ).reshape(NC, group, cols)
    mixture_own = lax.dynamic_index_in_dim(mixture, core, 0, keepdims=False)
    mixture_other = swap(lax.dynamic_index_in_dim(mixture, 1 - core, 0, keepdims=False))
    layer_out = full_residual + (mixture_own + mixture_other)
    return layer_out.astype(BF16).reshape(hidden.shape)


def split_mesh(mesh, nz):
    dev_count, y_count = mesh.devices.shape
    nx = dev_count // (NC * nz)
    return Mesh(mesh.devices.reshape(nx, nz, NC, y_count), ("x", "z", "c", "y"))


def solution(mesh, nz=8):
    dev = ("x", "z", "c")
    both = ("x", "z", "c", "y")
    in_specs = (
        P(dev, None, "y"),
        P(both, None, None, None),
        P(both, None, None),
        P(both, None, None),
        P(both),
        P(dev, None, None),
        P(dev, "y"),
        P("y"),
        P(dev, None, "y"),
        P(dev, None, "y"),
        P(dev, "y", None),
        P(dev, None, None),
        P(dev, None, None),
    )
    return jax.shard_map(
        on_device,
        mesh=split_mesh(mesh, nz),
        in_specs=in_specs,
        out_specs=P(dev, None, "y"),
        check_vma=False,
    )
```

```python
import jax
import jax.numpy as jnp
from jax import lax
from jax.sharding import Mesh, PartitionSpec as P

EPS = 1e-06
CAP = 4
NC = 2
F32 = jnp.float32
BF16 = jnp.bfloat16
CHIPS = ("x", "z")


def swap(value):
    return lax.ppermute(value, "c", [(0, 1), (1, 0)])


def send_y(value, distance):
    size = lax.axis_size("y")
    return lax.ppermute(value, "y", [(i, (i + distance) % size) for i in range(size)])


def in_core_order(core, own, other, axis=0):
    first = jnp.where(core == 0, own, other)
    second = jnp.where(core == 0, other, own)
    return jnp.concatenate([first, second], axis=axis)


def attend(queries, cache, new_latent, lengths, lat, scale):
    steps = queries.shape[1]
    scores = jnp.einsum("nshk,nck->nshc", queries, cache, preferred_element_type=F32) * scale
    fresh = jnp.einsum("nshk,njk->nshj", queries, new_latent, preferred_element_type=F32) * scale
    seen = jnp.arange(cache.shape[1])[None, :] < lengths[:, None]
    scores = jnp.where(seen[:, None, None, :], scores, -jnp.inf)
    known = jnp.arange(steps)[None, :] <= jnp.arange(steps)[:, None]
    fresh = jnp.where(known[None, :, None, :], fresh, -jnp.inf)
    top = jnp.maximum(jnp.max(scores, axis=-1), jnp.max(fresh, axis=-1))[..., None]
    scores = jnp.exp(scores - top)
    fresh = jnp.exp(fresh - top)
    total = (jnp.sum(scores, axis=-1) + jnp.sum(fresh, axis=-1))[..., None]
    old_part = jnp.einsum(
        "nshc,ncl->nshl", (scores / total).astype(BF16), cache[:, :, :lat], preferred_element_type=F32
    )
    new_part = jnp.einsum(
        "nshj,njl->nshl", (fresh / total).astype(BF16), new_latent[:, :, :lat], preferred_element_type=F32
    )
    return (old_part + new_part).astype(BF16)


def slots_of(ids):
    flat = ids.reshape(-1)
    order = jnp.arange(flat.shape[0])
    earlier = (flat[:, None] == flat[None, :]) & (order[None, :] < order[:, None])
    return jnp.sum(earlier.astype(jnp.int32), axis=1).reshape(ids.shape)


def on_device(
    hidden,
    queries,
    latent_cache,
    new_latent,
    lengths,
    value_proj,
    out_proj,
    norm_gain,
    w_gate,
    w_up,
    w_down,
    routes,
    route_gates,
):
    core = lax.axis_index("c")
    y = lax.axis_index("y")
    ny = lax.axis_size("y")
    chips = lax.axis_size("x") * lax.axis_size("z")
    rows, steps, heads, kv = queries.shape
    heads_core, lat, vdim = value_proj.shape
    rope = kv - lat
    cols = hidden.shape[2]
    half = cols // NC
    units = w_gate.shape[2]
    width = cols * ny
    own_tokens = rows * steps
    group = own_tokens * ny
    heads_chip = heads_core * NC
    slots = chips * NC * CAP
    near = (1, ny - 1)
    far = tuple(d for d in range(1, ny) if d not in near)

    def half_of(value, which):
        return lax.dynamic_slice_in_dim(value, which * half, half, value.ndim - 1)

    def after(value, done):
        return lax.optimization_barrier((value, done))[0]

    def over_chips(value):
        return lax.all_to_all(value, CHIPS, 0, 0, tiled=True)

    def down_block(block):
        return lax.dynamic_slice_in_dim(w_down[0], (block % ny) * cols, cols, 1)

    def row_block(weight, block):
        return lax.dynamic_slice_in_dim(weight[0], (block % ny) * cols, cols, 0)

    def up_block(block):
        return jnp.concatenate([row_block(w_gate, block), row_block(w_up, block)], axis=1)

    def half_block(block, which):
        start = (block % ny) * cols + which * half
        return jnp.concatenate(
            [lax.dynamic_slice_in_dim(weight[0], start, half, 0) for weight in (w_gate, w_up)],
            axis=1,
        )

    near_down = {d: send_y(down_block(y + d), d) for d in near}
    near_up = {d: up_block(y + d) for d in near}
    far_gain = {d: send_y(norm_gain, d) for d in far}

    vp = in_core_order(core, value_proj, swap(value_proj))
    op = in_core_order(core, half_of(out_proj, core), swap(half_of(out_proj, 1 - core)))
    flat_hidden = hidden.reshape(group, cols)
    chip_hidden = in_core_order(
        core, half_of(flat_hidden, core)[None], swap(half_of(flat_hidden, 1 - core))[None]
    )
    ids = routes.reshape(group, -1)
    gates = route_gates.reshape(group, -1)
    chip_ids = in_core_order(core, ids[None], swap(ids)[None])
    chip_gates = in_core_order(core, gates[None], swap(gates)[None]).astype(F32)

    context = attend(queries, latent_cache, new_latent, lengths, lat, (vdim + rope) ** (-0.5))
    context = context.reshape(own_tokens, chips, heads_chip, lat).transpose(1, 0, 2, 3)
    context = over_chips(context)
    context, near_down, near_up, vp, op, far_gain = lax.optimization_barrier(
        (context, near_down, near_up, vp, op, far_gain)
    )
    values = jnp.einsum("nthl,hlv->nthv", context, vp, preferred_element_type=F32).astype(BF16)

    values = jnp.concatenate([values] + [send_y(values, d) for d in range(1, ny)], axis=1)
    up_parts = {d: send_y(block, d) for d, block in after(near_up, values).items()}
    values = values.reshape(chips, group, heads_chip * vdim)
    values = jnp.concatenate([values, swap(values)], axis=1)
    sums = jnp.dot(
        values.reshape(-1, heads_chip * vdim), op, preferred_element_type=F32
    ).astype(BF16)
    sums = over_chips(sums.reshape(chips, NC * group, half))
    sums = jnp.sum(sums.astype(F32), axis=0).astype(BF16).astype(F32)

    core_order = (core + jnp.arange(NC)) % NC
    y_order = (y - jnp.arange(ny)) % ny
    token = jnp.arange(own_tokens)
    place = core_order[:, None, None] * group + y_order[None, :, None] * own_tokens + token
    place = place.reshape(-1)
    placed_hidden = chip_hidden.reshape(NC * group, half)[place].astype(F32)
    gain = half_of(norm_gain, core)

    chip_slots = jnp.stack([slots_of(chip_ids[0]), slots_of(chip_ids[1])])
    group_of = jnp.arange(NC)[:, None, None]
    row_of = ((chip_ids ^ core) * NC + group_of) * CAP + chip_slots
    row_of = row_of.reshape(NC * group, -1)
    row_ids = jnp.arange(chips * NC * NC * CAP)[None, None, :]
    named = row_of[:, :, None] == row_ids
    weighted = named.astype(F32) * chip_gates.reshape(NC * group, -1)[:, :, None]
    combine = jnp.sum(weighted, axis=1).astype(BF16).reshape(NC * group, chips, NC, NC * CAP)
    combine = combine[:, :, 0]
    spread = jnp.sum((row_of[place][:, :, None] == row_ids).astype(F32), axis=1).astype(BF16)

    residual = placed_hidden + sums
    scaled = (residual * gain).astype(BF16)
    far_down = {d: send_y(after(down_block(y + d), up_parts), d) for d in far}
    outgoing = lax.dot_general(
        spread, scaled, (((0,), (0,)), ((), ())), preferred_element_type=F32
    ).astype(BF16)
    tokens = over_chips(outgoing.reshape(chips, NC * NC * CAP, half))
    tokens = tokens.reshape(chips, NC, NC * CAP, half)
    kept, given = tokens[:, 0].reshape(slots, half), tokens[:, 1].reshape(slots, half)
    received = swap(given)
    kept, far_down = lax.optimization_barrier((kept, far_down))
    far_tokens = {d: (send_y(kept, d), swap(send_y(given, d))) for d in far}
    down_all = [down_block(y)] + [near_down[d] for d in near] + [far_down[d] for d in far]
    down_all = jnp.concatenate(down_all, axis=0)
    tokens = in_core_order(core, kept, received, axis=1)

    residual = residual.reshape(NC, group, half)
    full_residual = in_core_order(core, residual[0], swap(residual[1]), axis=1)
    back = (y - jnp.arange(ny)) % ny
    full_residual = full_residual.reshape(ny, own_tokens, cols)[back].reshape(group, cols)

    def share(part, gains):
        return jnp.sum(jnp.square(part.astype(F32) / gains), axis=1)

    own_share = share(tokens, norm_gain)
    squares = own_share
    sums = jnp.dot(tokens, up_block(y), preferred_element_type=F32)
    for d in near:
        part = jnp.dot(tokens, up_parts[d], preferred_element_type=F32)
        sums = sums + send_y(part.astype(BF16), -d).astype(F32)
        squares = squares + send_y(own_share, -d)
    for d in far:
        for part, which in zip(far_tokens[d], (core, 1 - core)):
            sums = sums + jnp.dot(part, half_block(y - d, which), preferred_element_type=F32)
            squares = squares + share(part, half_of(far_gain[d], which))
    sums = sums * lax.rsqrt(squares / width + EPS)[:, None]
    act = (jax.nn.silu(sums[:, :units]) * sums[:, units:]).astype(BF16)
    acts = jnp.concatenate([act] + [send_y(act, d) for d in near + far], axis=1)
    result = jnp.dot(acts, down_all, preferred_element_type=F32)
    result = result.astype(BF16).reshape(chips, NC * CAP, cols)

    returned = over_chips(result).reshape(slots, cols)
    mixture = jnp.dot(
        combine.reshape(NC * group, slots), returned, preferred_element_type=F32
    ).reshape(NC, group, cols)
    mixture_own = lax.dynamic_index_in_dim(mixture, core, 0, keepdims=False)
    mixture_other = swap(lax.dynamic_index_in_dim(mixture, 1 - core, 0, keepdims=False))
    layer_out = full_residual + (mixture_own + mixture_other)
    return layer_out.astype(BF16).reshape(hidden.shape)


def split_mesh(mesh, nz):
    dev_count, y_count = mesh.devices.shape
    nx = dev_count // (NC * nz)
    return Mesh(mesh.devices.reshape(nx, nz, NC, y_count), ("x", "z", "c", "y"))


def solution(mesh, nz=8):
    dev = ("x", "z", "c")
    both = ("x", "z", "c", "y")
    in_specs = (
        P(dev, None, "y"),
        P(both, None, None, None),
        P(both, None, None),
        P(both, None, None),
        P(both),
        P(dev, None, None),
        P(dev, "y"),
        P("y"),
        P(dev, None, "y"),
        P(dev, None, "y"),
        P(dev, "y", None),
        P(dev, None, None),
        P(dev, None, None),
    )
    return jax.shard_map(
        on_device,
        mesh=split_mesh(mesh, nz),
        in_specs=in_specs,
        out_specs=P(dev, None, "y"),
        check_vma=False,
    )
```

```python
import jax
import jax.numpy as jnp
from jax import lax
from jax.sharding import Mesh, PartitionSpec as P

EPS = 1e-06
CAP = 4
NC = 2
F32 = jnp.float32
BF16 = jnp.bfloat16
CHIPS = ("x", "z")


def swap(value):
    return lax.ppermute(value, "c", [(0, 1), (1, 0)])


def send_y(value, distance):
    size = lax.axis_size("y")
    return lax.ppermute(value, "y", [(i, (i + distance) % size) for i in range(size)])


def in_core_order(core, own, other, axis=0):
    first = jnp.where(core == 0, own, other)
    second = jnp.where(core == 0, other, own)
    return jnp.concatenate([first, second], axis=axis)


def attend(queries, cache, new_latent, lengths, lat, scale):
    steps = queries.shape[1]
    scores = jnp.einsum("nshk,nck->nshc", queries, cache, preferred_element_type=F32) * scale
    fresh = jnp.einsum("nshk,njk->nshj", queries, new_latent, preferred_element_type=F32) * scale
    seen = jnp.arange(cache.shape[1])[None, :] < lengths[:, None]
    scores = jnp.where(seen[:, None, None, :], scores, -jnp.inf)
    known = jnp.arange(steps)[None, :] <= jnp.arange(steps)[:, None]
    fresh = jnp.where(known[None, :, None, :], fresh, -jnp.inf)
    top = jnp.maximum(jnp.max(scores, axis=-1), jnp.max(fresh, axis=-1))[..., None]
    scores = jnp.exp(scores - top)
    fresh = jnp.exp(fresh - top)
    total = (jnp.sum(scores, axis=-1) + jnp.sum(fresh, axis=-1))[..., None]
    old_part = jnp.einsum(
        "nshc,ncl->nshl", (scores / total).astype(BF16), cache[:, :, :lat], preferred_element_type=F32
    )
    new_part = jnp.einsum(
        "nshj,njl->nshl", (fresh / total).astype(BF16), new_latent[:, :, :lat], preferred_element_type=F32
    )
    return (old_part + new_part).astype(BF16)


def slots_of(ids):
    flat = ids.reshape(-1)
    order = jnp.arange(flat.shape[0])
    earlier = (flat[:, None] == flat[None, :]) & (order[None, :] < order[:, None])
    return jnp.sum(earlier.astype(jnp.int32), axis=1).reshape(ids.shape)


def on_device(
    hidden,
    queries,
    latent_cache,
    new_latent,
    lengths,
    value_proj,
    out_proj,
    norm_gain,
    w_gate,
    w_up,
    w_down,
    routes,
    route_gates,
):
    core = lax.axis_index("c")
    y = lax.axis_index("y")
    ny = lax.axis_size("y")
    chips = lax.axis_size("x") * lax.axis_size("z")
    rows, steps, heads, kv = queries.shape
    heads_core, lat, vdim = value_proj.shape
    rope = kv - lat
    cols = hidden.shape[2]
    half = cols // NC
    units = w_gate.shape[2]
    width = cols * ny
    own_tokens = rows * steps
    group = own_tokens * ny
    heads_chip = heads_core * NC
    slots = chips * NC * CAP
    near = (1, ny - 1)
    far = tuple(d for d in range(1, ny) if d not in near)

    def half_of(value, which):
        return lax.dynamic_slice_in_dim(value, which * half, half, value.ndim - 1)

    def after(value, done):
        return lax.optimization_barrier((value, done))[0]

    def over_chips(value):
        return lax.all_to_all(value, CHIPS, 0, 0, tiled=True)

    def down_block(block):
        return lax.dynamic_slice_in_dim(w_down[0], (block % ny) * cols, cols, 1)

    def row_block(weight, block):
        return lax.dynamic_slice_in_dim(weight[0], (block % ny) * cols, cols, 0)

    def up_block(block):
        return jnp.concatenate([row_block(w_gate, block), row_block(w_up, block)], axis=1)

    def half_block(block, which):
        start = (block % ny) * cols + which * half
        return jnp.concatenate(
            [lax.dynamic_slice_in_dim(weight[0], start, half, 0) for weight in (w_gate, w_up)],
            axis=1,
        )

    near_down = {d: send_y(down_block(y + d), d) for d in near}
    near_up = {d: up_block(y + d) for d in near}
    far_gain = {d: send_y(norm_gain, d) for d in far}

    vp = in_core_order(core, value_proj, swap(value_proj))
    op = in_core_order(core, half_of(out_proj, core), swap(half_of(out_proj, 1 - core)))
    flat_hidden = hidden.reshape(group, cols)
    chip_hidden = in_core_order(
        core, half_of(flat_hidden, core)[None], swap(half_of(flat_hidden, 1 - core))[None]
    )
    ids = routes.reshape(group, -1)
    gates = route_gates.reshape(group, -1)
    chip_ids = in_core_order(core, ids[None], swap(ids)[None])
    chip_gates = in_core_order(core, gates[None], swap(gates)[None]).astype(F32)

    context = attend(queries, latent_cache, new_latent, lengths, lat, (vdim + rope) ** (-0.5))
    context = context.reshape(own_tokens, chips, heads_chip, lat).transpose(1, 0, 2, 3)
    context = over_chips(context)
    context, near_down, near_up, vp, op, far_gain = lax.optimization_barrier(
        (context, near_down, near_up, vp, op, far_gain)
    )
    values = jnp.einsum("nthl,hlv->nthv", context, vp, preferred_element_type=F32).astype(BF16)

    values = jnp.concatenate([values] + [send_y(values, d) for d in range(1, ny)], axis=1)
    up_parts = {d: send_y(block, d) for d, block in after(near_up, values).items()}
    values = values.reshape(chips, group, heads_chip * vdim)
    values = jnp.concatenate([values, swap(values)], axis=1)
    sums = jnp.dot(
        values.reshape(-1, heads_chip * vdim), op, preferred_element_type=F32
    ).astype(BF16)
    sums = over_chips(sums.reshape(chips, NC * group, half))
    sums = jnp.sum(sums.astype(F32), axis=0).astype(BF16).astype(F32)

    core_order = (core + jnp.arange(NC)) % NC
    y_order = (y - jnp.arange(ny)) % ny
    token = jnp.arange(own_tokens)
    place = core_order[:, None, None] * group + y_order[None, :, None] * own_tokens + token
    place = place.reshape(-1)
    placed_hidden = chip_hidden.reshape(NC * group, half)[place].astype(F32)
    gain = half_of(norm_gain, core)

    chip_slots = jnp.stack([slots_of(chip_ids[0]), slots_of(chip_ids[1])])
    group_of = jnp.arange(NC)[:, None, None]
    row_of = ((chip_ids ^ core) * NC + group_of) * CAP + chip_slots
    row_of = row_of.reshape(NC * group, -1)
    row_ids = jnp.arange(chips * NC * NC * CAP)[None, None, :]
    named = row_of[:, :, None] == row_ids
    weighted = named.astype(F32) * chip_gates.reshape(NC * group, -1)[:, :, None]
    combine = jnp.sum(weighted, axis=1).astype(BF16).reshape(NC * group, chips, NC, NC * CAP)
    combine = combine[:, :, 0]
    spread = jnp.sum((row_of[place][:, :, None] == row_ids).astype(F32), axis=1).astype(BF16)

    residual = placed_hidden + sums
    scaled = (residual * gain).astype(BF16)
    far_down = {d: send_y(after(down_block(y + d), up_parts), d) for d in far}
    outgoing = lax.dot_general(
        spread, scaled, (((0,), (0,)), ((), ())), preferred_element_type=F32
    ).astype(BF16)
    tokens = over_chips(outgoing.reshape(chips, NC * NC * CAP, half))
    tokens = tokens.reshape(chips, NC, NC * CAP, half)
    tokens, far_down = lax.optimization_barrier((tokens, far_down))
    far_arrived = {d: send_y(tokens, d) for d in far}

    def split(value):
        return value[:, 0].reshape(slots, half), swap(value[:, 1].reshape(slots, half))

    kept, received = split(tokens)
    far_tokens = {d: split(far_arrived[d]) for d in far}
    down_all = [down_block(y)] + [near_down[d] for d in near] + [far_down[d] for d in far]
    down_all = jnp.concatenate(down_all, axis=0)
    tokens = in_core_order(core, kept, received, axis=1)

    residual = residual.reshape(NC, group, half)
    full_residual = in_core_order(core, residual[0], swap(residual[1]), axis=1)
    back = (y - jnp.arange(ny)) % ny
    full_residual = full_residual.reshape(ny, own_tokens, cols)[back].reshape(group, cols)

    def share(part, gains):
        return jnp.sum(jnp.square(part.astype(F32) / gains), axis=1)

    own_share = share(tokens, norm_gain)
    squares = own_share
    sums = jnp.dot(tokens, up_block(y), preferred_element_type=F32)
    for d in near:
        part = jnp.dot(tokens, up_parts[d], preferred_element_type=F32)
        sums = sums + send_y(part.astype(BF16), -d).astype(F32)
        squares = squares + send_y(own_share, -d)
    for d in far:
        for part, which in zip(far_tokens[d], (core, 1 - core)):
            sums = sums + jnp.dot(part, half_block(y - d, which), preferred_element_type=F32)
            squares = squares + share(part, half_of(far_gain[d], which))
    sums = sums * lax.rsqrt(squares / width + EPS)[:, None]
    act = (jax.nn.silu(sums[:, :units]) * sums[:, units:]).astype(BF16)
    acts = jnp.concatenate([act] + [send_y(act, d) for d in near + far], axis=1)
    result = jnp.dot(acts, down_all, preferred_element_type=F32)
    result = result.astype(BF16).reshape(chips, NC * CAP, cols)

    returned = over_chips(result).reshape(slots, cols)
    mixture = jnp.dot(
        combine.reshape(NC * group, slots), returned, preferred_element_type=F32
    ).reshape(NC, group, cols)
    mixture_own = lax.dynamic_index_in_dim(mixture, core, 0, keepdims=False)
    mixture_other = swap(lax.dynamic_index_in_dim(mixture, 1 - core, 0, keepdims=False))
    layer_out = full_residual + (mixture_own + mixture_other)
    return layer_out.astype(BF16).reshape(hidden.shape)


def split_mesh(mesh, nz):
    dev_count, y_count = mesh.devices.shape
    nx = dev_count // (NC * nz)
    return Mesh(mesh.devices.reshape(nx, nz, NC, y_count), ("x", "z", "c", "y"))


def solution(mesh, nz=8):
    dev = ("x", "z", "c")
    both = ("x", "z", "c", "y")
    in_specs = (
        P(dev, None, "y"),
        P(both, None, None, None),
        P(both, None, None),
        P(both, None, None),
        P(both),
        P(dev, None, None),
        P(dev, "y"),
        P("y"),
        P(dev, None, "y"),
        P(dev, None, "y"),
        P(dev, "y", None),
        P(dev, None, None),
        P(dev, None, None),
    )
    return jax.shard_map(
        on_device,
        mesh=split_mesh(mesh, nz),
        in_specs=in_specs,
        out_specs=P(dev, None, "y"),
        check_vma=False,
    )
```
